32 devices in a mesh: dp: 8 (over z, y), ctx: 4 (over x, core).
Axes of the slice: x: 2, y: 2, z: 4, core: 2. Of those that a mesh axis runs over, the one named last changes fastest.
Arguments:
- tokens: int32 [8, 512], P('dp', 'ctx'), may hold values from 0 to 511
- embedding: bfloat16 [512, 2048], replicated, may hold values from -6 to 6
- cotangent: bfloat16 [8, 512, 2048], P('dp', 'ctx'), may hold values from -6 to 6
- long_filter: float32 [128, 512], P('ctx'), may hold values from -1 to 1
- short_filter: float32 [3, 7, 2048], replicated, may hold values from -4 to 4
Outputs:
- block_output: bfloat16 [8, 512, 2048], P('dp', 'ctx')
- grad_input: bfloat16 [8, 512, 2048], P('dp', 'ctx')
- grad_long: float32 [128, 512], P('ctx')
- grad_short: float32 [3, 7, 2048], replicated
The draws below stay inside these ranges and needn't reach their ends.
All inputs are finite; a program needn't handle non-finite values.
Results may differ from the reference program's by a relative error of at most 0.0058.
Values may be sent and summed in bfloat16 or wider, within the bound.
A program may use at most 64 MiB of HBM per device.

```python
import math
import jax
import jax.numpy as jnp
import numpy as np
from jax import lax

C = 2048
GROUP = 16
SHORT = 7
VOCAB = 512
SEGMENT_LENGTH = 512
REPL = 8
FILTER_GROUPS = 128
N_DP = 8


def draw_long_filter(key, part):
    key_rough = jax.random.fold_in(key, 101)
    key_decay = jax.random.fold_in(key, 202)
    key_impulse = jax.random.fold_in(key, 303)
    rough_part = jnp.clip(jax.random.normal(key_rough, (FILTER_GROUPS, SEGMENT_LENGTH), jnp.float32), -4.0, 4.0)
    decay_len = jnp.exp(jax.random.uniform(key_decay, (FILTER_GROUPS, 1), jnp.float32, math.log(30.0), math.log(4.0 * SEGMENT_LENGTH)))
    impulse_trains = jax.random.randint(key_impulse, (FILTER_GROUPS, 3), 1, SEGMENT_LENGTH)
    token_places = jnp.arange(SEGMENT_LENGTH, dtype=jnp.int32)[None, :]
    carried_over = (token_places >= impulse_trains[:, 0:1]).astype(jnp.float32)
    carried_over = carried_over + (token_places >= impulse_trains[:, 1:2]).astype(jnp.float32)
    carried_over = carried_over + (token_places >= impulse_trains[:, 2:3]).astype(jnp.float32)
    decay_profile = jnp.exp(-token_places.astype(jnp.float32) / decay_len) * jnp.power(0.6, carried_over)
    amplitude = jax.lax.rsqrt(0.5 * jnp.minimum(decay_len, SEGMENT_LENGTH * 1.0) + 1.0)
    return rough_part * decay_profile * amplitude


def plant(entries, stream_key, smallest, top_value):
    spot = [jax.random.randint(jax.random.fold_in(stream_key, axis), (), 0, length) for axis, length in enumerate(entries.shape)]
    main_axis = entries.shape.index(max(entries.shape))
    beside = spot[:main_axis] + [(spot[main_axis] + 1) % entries.shape[main_axis]] + spot[main_axis + 1:]
    return entries.at[tuple(spot)].set(smallest).at[tuple(beside)].set(top_value)


def block_scale(stream_key, dims, shards, least, largest):
    loudness = 1.0
    for dim, blocks in shards:
        heights = jax.random.uniform(jax.random.fold_in(jax.random.fold_in(stream_key, 6), dim), (blocks,), jnp.float32, least / len(shards), largest / len(shards))
        loudness = loudness * jnp.repeat(jnp.exp(heights), dims[dim] // blocks).reshape((-1,) + (1,) * (len(dims) - 1 - dim))
    return loudness


def rank_bounds(count, lean):
    weights = [(1 << 20) // math.isqrt(rank ** lean) + 1 for rank in range(1, count + 1)]
    deviation = 1 + sum(weights) // (1 << 30)
    return np.cumsum(np.array([max(1, weight // deviation) for weight in weights]))


def skewed_ids(key, shape, number_of, lean):
    table = rank_bounds(number_of, lean)
    pick = jax.random.randint(jax.random.fold_in(key, 1), shape, 0, int(table[number_of - 1]))
    grade = jnp.searchsorted(jnp.asarray(table, jnp.int32), pick, side="right")
    return jax.random.permutation(jax.random.fold_in(key, 2), number_of)[grade].astype(jnp.int32)


def gaussian(own_key, extent, spread, most, split=(), kind=jnp.bfloat16):
    factor_of = block_scale(own_key, extent, split, -0.22, 0.18) if split else 1.0
    values = jax.random.normal(own_key, extent, jnp.float32) * spread * factor_of
    return jnp.minimum(jnp.maximum(values, -most), most).astype(kind)


def setup_inputs(seed: int = 0) -> dict:
    key_of = jax.random.split(jax.random.key(seed), 6)
    return {
        "tokens": plant(skewed_ids(key_of[0], (REPL, SEGMENT_LENGTH), VOCAB, 2), jax.random.fold_in(key_of[0], 3), 0, VOCAB - 1).astype(jnp.int32),
        "embedding": gaussian(key_of[1], (VOCAB, C), 1.0, 6.0),
        "cotangent": gaussian(key_of[2], (REPL, SEGMENT_LENGTH, C), 1.0, 6.0, ((0, 8), (1, 4))),
        "long_filter": draw_long_filter(jax.random.fold_in(key_of[5], 71), 0),
        "short_filter": gaussian(key_of[4], (3, SHORT, C), 0.38, 4.0, (), jnp.float32),
    }


def short_pass(padded, short_filter, stream, length):
    rim_width = SHORT - 1
    running = short_filter[stream, 0] * padded[rim_width:rim_width + length]
    for offset in range(1, SHORT):
        running = running + short_filter[stream, offset] * padded[rim_width - offset:rim_width - offset + length]
    return running


def reference(tokens, embedding, cotangent, long_filter, short_filter):
    rim_width = SHORT - 1
    grad_scale = 1.0 / (N_DP * GROUP)
    filter_spec = jnp.fft.rfft(long_filter.T, n=2 * SEGMENT_LENGTH, axis=0)
    filter_wide = jnp.repeat(filter_spec, GROUP, axis=1)

    def segment_step(running, inputs):
        segment_ids, seg_grad = inputs
        embedded = jnp.take(embedding, segment_ids, axis=0).astype(jnp.float32)
        padded = jnp.concatenate([jnp.zeros((rim_width, C), jnp.float32), embedded], axis=0)
        query_side = short_pass(padded, short_filter, 0, SEGMENT_LENGTH)
        key_side = short_pass(padded, short_filter, 1, SEGMENT_LENGTH)
        value_side = short_pass(padded, short_filter, 2, SEGMENT_LENGTH)
        gated_prod = (key_side * value_side).astype(jnp.bfloat16)
        gated_spec = jnp.fft.rfft(gated_prod.astype(jnp.float32), n=2 * SEGMENT_LENGTH, axis=0)
        conv_out = jnp.fft.irfft(gated_spec * filter_wide, n=2 * SEGMENT_LENGTH, axis=0)[:SEGMENT_LENGTH].astype(jnp.bfloat16)
        conv_float = conv_out.astype(jnp.float32)
        block_output = (query_side * conv_float).astype(jnp.bfloat16)
        grad_float = seg_grad.astype(jnp.float32)
        grad_conv = (grad_float * query_side).astype(jnp.bfloat16)
        grad_spec = jnp.fft.rfft(grad_conv.astype(jnp.float32), n=2 * SEGMENT_LENGTH, axis=0)
        grad_gated = jnp.fft.irfft(jnp.conj(filter_wide) * grad_spec, n=2 * SEGMENT_LENGTH, axis=0)[:SEGMENT_LENGTH].astype(jnp.bfloat16)
        cross_spec = (jnp.conj(gated_spec) * grad_spec).reshape(SEGMENT_LENGTH + 1, FILTER_GROUPS, GROUP).sum(axis=2)
        filter_term = jnp.fft.irfft(cross_spec, n=2 * SEGMENT_LENGTH, axis=0)[:SEGMENT_LENGTH].T * grad_scale
        gated_float = grad_gated.astype(jnp.float32)
        stream_grads = [grad_float * conv_float, gated_float * value_side, gated_float * key_side]
        grad_input = jnp.zeros((SEGMENT_LENGTH, C), jnp.float32)
        tap_rows = []
        for stream in range(3):
            tail = jnp.concatenate([stream_grads[stream], jnp.zeros((rim_width, C), jnp.float32)], axis=0)
            for offset in range(SHORT):
                grad_input = grad_input + short_filter[stream, offset] * tail[offset:offset + SEGMENT_LENGTH]
                tap_rows.append(jnp.sum(stream_grads[stream] * padded[rim_width - offset:rim_width - offset + SEGMENT_LENGTH], axis=0))
        taps_term = jnp.stack(tap_rows).reshape(3, SHORT, C) * grad_scale
        return (running[0] + filter_term, running[1] + taps_term), (block_output, grad_input.astype(jnp.bfloat16))

    start = (jnp.zeros((FILTER_GROUPS, SEGMENT_LENGTH), jnp.float32), jnp.zeros((3, SHORT, C), jnp.float32))
    totals, results = lax.scan(segment_step, start, (tokens, cotangent))
    return (results[0], results[1], totals[0], totals[1])
```

```python
import functools

import jax
import jax.numpy as jnp
from jax import lax
from jax.experimental import pallas as pl
from jax.experimental.pallas import tpu as pltpu
from jax.sharding import PartitionSpec as P

LANES = 128
F32 = jnp.float32
BF16 = jnp.bfloat16


def contract(a, b, da, db):
    return lax.dot_general(a, b, (((da,), (db,)), ((), ())), preferred_element_type=F32)


def kernel(taps, scale, tok_ref, emb_ref, cot_ref, h_ref, w_ref,
           blk_ref, gin_ref, long_ref, short_ref,
           hot, e_t, cot_t, blk_t, gin_t):
    vocab = emb_ref.shape[0]
    length, chans = cot_ref.shape
    groups = h_ref.shape[0]
    group = chans // groups
    n = length // LANES

    ids = lax.broadcasted_iota(jnp.int32, (vocab, length), 0)
    hot[...] = (ids == tok_ref[...]).astype(F32).astype(BF16)

    @pl.loop(0, chans // LANES)
    def _(c):
        cs = pl.ds(pl.multiple_of(c * LANES, LANES), LANES)
        e_t[cs, :] = contract(emb_ref[:, cs], hot[...], 0, 0)
        cot_t[cs, :] = cot_ref[:, cs].astype(F32).T

    @pl.loop(0, groups)
    def _(g):
        rows = pl.ds(pl.multiple_of(g * group, group), group)
        lane = lax.broadcasted_iota(jnp.int32, (group, length), 1)
        e = e_t[rows, :]
        es = [e] + [jnp.where(lane >= j, pltpu.roll(e, j, 1), 0.0) for j in range(1, taps)]
        w = w_ref[rows, :]
        col = [w[:, k:k + 1] for k in range(3 * taps)]

        def stream(s):
            total = col[s * taps] * es[0]
            for j in range(1, taps):
                total = total + col[s * taps + j] * es[j]
            return total

        q, k, v = stream(0), stream(1), stream(2)
        cot = cot_t[rows, :]
        x = (k * v).astype(BF16)
        gc = (cot * q).astype(BF16)
        xb = [x[:, i * LANES:(i + 1) * LANES] for i in range(n)]
        gb = [gc[:, i * LANES:(i + 1) * LANES] for i in range(n)]
        zero = jnp.zeros((group, LANES), BF16)
        lx = jnp.concatenate(
            [jnp.concatenate([xb[i - d] if d <= i else zero for d in range(n)], axis=1)
             for i in range(n)], axis=0)
        lg = jnp.concatenate(
            [jnp.concatenate([gb[i + d] if i + d < n else zero for d in range(n)], axis=1)
             for i in range(n)], axis=0)
        xs = jnp.concatenate(xb, axis=0)

        h = h_ref[pl.ds(g, 1), :]
        sub_i = lax.broadcasted_iota(jnp.int32, (LANES, LANES), 0)
        lane_i = lax.broadcasted_iota(jnp.int32, (LANES, LANES), 1)
        upper = lane_i >= sub_i
        prev = jnp.zeros((LANES, LANES), F32)
        ws = []
        for d in range(n):
            part = jnp.broadcast_to(h[:, d * LANES:(d + 1) * LANES], (LANES, LANES))
            turned = pltpu.roll(part, 0, 1, stride=1, stride_axis=0)
            ws.append(jnp.where(upper, turned, prev).astype(BF16))
            prev = turned
        conv = contract(lx, jnp.concatenate(ws, axis=0), 1, 0)
        gg = contract(lg, jnp.concatenate(ws, axis=1), 1, 1)
        cross = contract(xs, lg, 0, 0)

        def wide(a):
            return jnp.concatenate([a[i * group:(i + 1) * group] for i in range(n)], axis=1)

        cross = jnp.concatenate(
            [jnp.where(upper, cross[:, :LANES], 0.0), cross[:, LANES:]], axis=1)
        size = LANES
        while size > 8:
            size //= 2
            cross = cross[:size] + pltpu.roll(cross[size:], length - size, 1)
        while size > 1:
            size //= 2
            cross = cross + pltpu.roll(pltpu.roll(cross, 8 - size, 0), length - size, 1)
        long_ref[pl.ds(g, 1), :] = cross[0:1] * scale

        cb = wide(conv).astype(BF16).astype(F32)
        gb2 = wide(gg).astype(BF16).astype(F32)
        blk_t[rows, :] = q * cb
        grads = [cot * cb, gb2 * v, gb2 * k]
        total = None
        for j in range(taps - 1, -1, -1):
            term = (col[j] * grads[0] + col[taps + j] * grads[1]
                    + col[2 * taps + j] * grads[2])
            if total is not None:
                term = term + jnp.where(lane < length - 1, pltpu.roll(total, length - 1, 1), 0.0)
            total = term
        gin_t[rows, :] = total

        lane_k = lax.broadcasted_iota(jnp.int32, (group, LANES), 1)
        acc = jnp.zeros((group, LANES), F32)
        for s in range(3):
            for j in range(taps):
                prod = grads[s] * es[j]
                fold = prod[:, :LANES]
                for i in range(1, n):
                    fold = fold + prod[:, i * LANES:(i + 1) * LANES]
                acc = jnp.where(lane_k == s * taps + j, jnp.sum(fold, axis=1, keepdims=True), acc)
        short_ref[rows, :] = acc * scale

    @pl.loop(0, chans // LANES)
    def _(c):
        cs = pl.ds(pl.multiple_of(c * LANES, LANES), LANES)
        blk_ref[:, cs] = blk_t[cs, :].T.astype(BF16)
        gin_ref[:, cs] = gin_t[cs, :].T.astype(BF16)


def on_device(tokens, embedding, cotangent, long_filter, short_filter):
    streams, taps, channels = short_filter.shape
    vocab = embedding.shape[0]
    n_ctx = lax.axis_size("ctx")
    n_dp = lax.axis_size("dp")
    me = lax.axis_index("ctx")
    chans = channels // n_ctx
    groups, length = long_filter.shape
    scale = 1.0 / (n_dp * (chans // groups))

    ids = lax.all_gather(tokens, "ctx", axis=1, tiled=True)
    emb = lax.dynamic_slice(embedding, (0, me * chans), (vocab, chans))
    w = lax.dynamic_slice(short_filter.reshape(streams * taps, channels), (0, me * chans),
                          (streams * taps, chans))
    w = jnp.pad(w.T, ((0, 0), (0, LANES - streams * taps)))
    cot = lax.all_to_all(cotangent, "ctx", split_axis=2, concat_axis=1, tiled=True)[0]
    vmem = pl.BlockSpec(memory_space=pltpu.VMEM)
    blk, gin, long_part, short_part = pl.pallas_call(
        functools.partial(kernel, taps, scale),
        out_shape=[
            jax.ShapeDtypeStruct((length, chans), BF16),
            jax.ShapeDtypeStruct((length, chans), BF16),
            jax.ShapeDtypeStruct((groups, length), F32),
            jax.ShapeDtypeStruct((chans, LANES), F32),
        ],
        in_specs=[vmem] * 5,
        out_specs=[vmem] * 4,
        scratch_shapes=[
            pltpu.VMEM((vocab, length), BF16),
            pltpu.VMEM((chans, length), F32),
            pltpu.VMEM((chans, length), F32),
            pltpu.VMEM((chans, length), F32),
            pltpu.VMEM((chans, length), F32),
        ],
        compiler_params=pltpu.CompilerParams(vmem_limit_bytes=48 * 1024 * 1024),
        name="hyena",
    )(ids, emb, cot, long_filter, w)
    both = jnp.stack([blk, gin])
    both = lax.all_to_all(both, "ctx", split_axis=1, concat_axis=2, tiled=True)
    grad_long = lax.psum(long_part, "dp")
    short_part = short_part[:, :streams * taps].T
    short_sum = lax.psum(short_part, "dp")
    grad_short = lax.all_gather(short_sum, "ctx", axis=1, tiled=True)
    return (both[0:1], both[1:2], grad_long, grad_short.reshape(streams, taps, channels))


def solution(mesh):
    in_specs = (P("dp", "ctx"), P(), P("dp", "ctx", None), P("ctx", None), P())
    out_specs = (P("dp", "ctx", None), P("dp", "ctx", None), P("ctx", None), P())
    return jax.shard_map(
        on_device, mesh=mesh, in_specs=in_specs, out_specs=out_specs, check_vma=False
    )
```

```python
import jax
import jax.numpy as jnp
from jax import lax
from jax.experimental import pallas as pl
from jax.experimental.pallas import tpu as pltpu
from jax.sharding import PartitionSpec as P

LANES = 128
F32 = jnp.float32
BF16 = jnp.bfloat16
MESH = pl.DeviceIdType.MESH


def contract(a, b, da, db):
    return lax.dot_general(a, b, (((da,), (db,)), ((), ())), preferred_element_type=F32)


def kernel(tok_ref, emb_ref, cot_ref, h_ref, w_ref,
           blk_ref, gin_ref, long_ref, short_ref,
           ids, emb, cot_b, hot, e_t, cot_t, blk_t, gin_t, w_s, w_t, blk_s, gin_s,
           long_s, short_t, red, got, summed, short_b,
           emb_sem, own_sem, out_sem, tok_send, tok_recv, cot_send, cot_recv,
           res_send, res_recv, red_send, red_recv, sum_send, sum_recv, sh_send, sh_recv):
    n_ctx, n_dp = lax.axis_size("ctx"), lax.axis_size("dp")
    me, mine = lax.axis_index("ctx"), lax.axis_index("dp")
    vocab, chans = emb.shape
    taps = w_ref.shape[1]
    groups, length = h_ref.shape
    group = chans // groups
    n = length // LANES
    own_len = tok_ref.shape[1]
    chunks = chans // LANES
    scale = 1.0 / (n_dp * group)
    per = got.shape[1]
    where = pl.ds(pl.multiple_of(me * chans, chans), chans)

    def ctx(k):
        return lax.rem(me + k, n_ctx)

    def dp(k):
        return lax.rem(mine + k, n_dp)

    def remote(src, dst, send, recv, target):
        return pltpu.make_async_remote_copy(
            src_ref=src, dst_ref=dst, send_sem=send, recv_sem=recv,
            device_id=target, device_id_type=MESH)

    emb_copy = pltpu.make_async_copy(emb_ref.at[:, where], emb, emb_sem)
    emb_copy.start()

    def cot_part(p, c):
        return cot_ref.at[0, :, pl.ds(pl.multiple_of(p * chans + c * LANES, LANES), LANES)]

    def own_cot(c):
        return pltpu.make_async_copy(cot_part(me, c), cot_b.at[c, me], own_sem.at[c])

    for c in range(chunks):
        own_cot(c).start()

    barrier = pltpu.get_barrier_semaphore()
    for k in range(1, n_ctx):
        pl.semaphore_signal(barrier, inc=1, device_id={"ctx": ctx(k)}, device_id_type=MESH)

    @pl.loop(1, n_dp)
    def _(k):
        pl.semaphore_signal(barrier, inc=1, device_id={"dp": dp(k)}, device_id_type=MESH)

    pl.semaphore_wait(barrier, n_ctx + n_dp - 2)

    def tok_copy(k, slot):
        return remote(tok_ref, ids.at[slot], tok_send.at[k], tok_recv.at[k], {"ctx": ctx(k)})

    def cot_copy(k, c, slot):
        return remote(cot_part(ctx(k), c), cot_b.at[c, slot],
                      cot_send.at[c, k], cot_recv.at[c, k], {"ctx": ctx(k)})

    for k in range(1, n_ctx):
        tok_copy(k, me).start()
    for c in range(chunks):
        for k in range(1, n_ctx):
            cot_copy(k, c, me).start()
    ids[me] = tok_ref[...]

    w_s[...] = jnp.zeros_like(w_s)
    for s in range(3):
        w_s[s * 8:s * 8 + taps, :] = w_ref[s, :, where]
    for c in range(chunks):
        w_t[c * LANES:(c + 1) * LANES, :] = w_s[:, c * LANES:(c + 1) * LANES].T
    if red.shape[0] > (groups // 8) * n + 3 * chunks:
        red[...] = jnp.zeros_like(red)

    for k in range(1, n_ctx):
        tok_copy(k, ctx(n_ctx - k)).wait()
    rows_v = lax.broadcasted_iota(jnp.int32, (vocab, own_len), 0)
    for i in range(n_ctx):
        hot[:, i * own_len:(i + 1) * own_len] = (rows_v == ids[i]).astype(F32).astype(BF16)
    emb_copy.wait()

    sub_i = lax.broadcasted_iota(jnp.int32, (LANES, LANES), 0)
    lane_i = lax.broadcasted_iota(jnp.int32, (LANES, LANES), 1)
    upper = lane_i >= sub_i
    lane = lax.broadcasted_iota(jnp.int32, (group, length), 1)
    lane_k = lax.broadcasted_iota(jnp.int32, (group, LANES), 1)

    def first(g):
        rows = pl.ds(pl.multiple_of(g * group, group), group)
        e = e_t[rows, :]
        es = [e] + [jnp.where(lane >= j, pltpu.roll(e, j, 1), 0.0) for j in range(1, taps)]
        w = w_t[rows, :]
        col = [[w[:, s * 8 + j:s * 8 + j + 1] for j in range(taps)] for s in range(3)]

        def stream(s):
            total = col[s][0] * es[0]
            for j in range(1, taps):
                total = total + col[s][j] * es[j]
            return total

        q, k, v = stream(0), stream(1), stream(2)
        cot = cot_t[rows, :]
        x = (k * v).astype(BF16)
        gc = (cot * q).astype(BF16)
        return rows, es, col, q, k, v, cot, x, gc

    def second(g, x, gc):
        xb = [x[:, i * LANES:(i + 1) * LANES] for i in range(n)]
        gb = [gc[:, i * LANES:(i + 1) * LANES] for i in range(n)]
        zero = jnp.zeros((group, LANES), BF16)
        lx = jnp.concatenate(
            [jnp.concatenate([xb[i - d] if d <= i else zero for d in range(n)], axis=1)
             for i in range(n)], axis=0)
        lg = jnp.concatenate(
            [jnp.concatenate([gb[i + d] if i + d < n else zero for d in range(n)], axis=1)
             for i in range(n)], axis=0)
        xs = jnp.concatenate(xb, axis=0)
        h = h_ref[pl.ds(g, 1), :]
        prev = jnp.zeros((LANES, LANES), F32)
        ws = []
        for d in range(n):
            part = jnp.broadcast_to(h[:, d * LANES:(d + 1) * LANES], (8, LANES))
            base = pltpu.roll(part, 0, 1, stride=1, stride_axis=0)
            turned = jnp.concatenate(
                [base] + [pltpu.roll(base, m, 1) for m in range(8, LANES, 8)], axis=0)
            ws.append(jnp.where(upper, turned, prev).astype(BF16))
            prev = turned
        conv = contract(lx, jnp.concatenate(ws, axis=0), 1, 0)
        gg = contract(lg, jnp.concatenate(ws, axis=1), 1, 1)
        cross = contract(xs, lg, 0, 0)
        return conv, gg, cross

    def wide(a):
        return jnp.concatenate([a[i * group:(i + 1) * group] for i in range(n)], axis=1)

    def third(g, rows, es, col, q, k, v, cot, conv, gg, cross):
        cross = jnp.concatenate(
            [jnp.where(upper, cross[:, :LANES], 0.0), cross[:, LANES:]], axis=1)
        size = LANES
        while size > 8:
            size //= 2
            cross = cross[:size] + pltpu.roll(cross[size:], length - size, 1)
        while size > 1:
            size //= 2
            cross = cross + pltpu.roll(pltpu.roll(cross, 8 - size, 0), length - size, 1)
        long_s[pl.ds(g, 1), :] = cross[0:1] * scale

        cb = wide(conv).astype(BF16).astype(F32)
        gb2 = wide(gg).astype(BF16).astype(F32)
        blk_t[rows, :] = q * cb
        grads = [cot * cb, gb2 * v, gb2 * k]
        total = None
        for j in range(taps - 1, -1, -1):
            term = col[0][j] * grads[0] + col[1][j] * grads[1] + col[2][j] * grads[2]
            if total is not None:
                term = term + jnp.where(lane < length - 1, pltpu.roll(total, length - 1, 1), 0.0)
            total = term
        gin_t[rows, :] = total
        acc = jnp.zeros((group, LANES), F32)
        for s in range(3):
            for j in range(taps):
                prod = grads[s] * es[j]
                fold = prod[:, :LANES]
                for i in range(1, n):
                    fold = fold + prod[:, i * LANES:(i + 1) * LANES]
                acc = jnp.where(lane_k == s * 8 + j, jnp.sum(fold, axis=1, keepdims=True), acc)
        short_t[rows, :] = acc * scale

    def results(c, k):
        at = pl.ds(pl.multiple_of(me * chans + c * LANES, LANES), LANES)
        to = ctx(k)
        return [remote(src.at[c, to], dst.at[0, :, at], res_send.at[i, c, k],
                       res_recv.at[i, c, k], {"ctx": to})
                for i, (src, dst) in enumerate(((blk_s, blk_ref), (gin_s, gin_ref)))]

    def arrivals(c, k):
        src_dev = ctx(n_ctx - k)
        at = pl.ds(pl.multiple_of(src_dev * chans + c * LANES, LANES), LANES)
        return [remote(src.at[c, me], dst.at[0, :, at], res_send.at[i, c, k],
                       res_recv.at[i, c, k], {"ctx": ctx(k)})
                for i, (src, dst) in enumerate(((blk_s, blk_ref), (gin_s, gin_ref)))]

    def own_results(c):
        at = pl.ds(pl.multiple_of(me * chans + c * LANES, LANES), LANES)
        return [pltpu.make_async_copy(src.at[c, me], dst.at[0, :, at], out_sem.at[i, c])
                for i, (src, dst) in enumerate(((blk_s, blk_ref), (gin_s, gin_ref)))]

    in_chunk = LANES // group
    step = 2 if in_chunk % 2 == 0 else 1

    @pl.loop(0, chunks)
    def _(c):
        cs = pl.ds(pl.multiple_of(c * LANES, LANES), LANES)
        e_t[cs, :] = contract(emb[:, cs], hot[...], 0, 0)
        own_cot(c).wait()
        for k in range(1, n_ctx):
            cot_copy(k, c, ctx(n_ctx - k)).wait()
        for i in range(n_ctx):
            cot_t[cs, i * own_len:(i + 1) * own_len] = cot_b[c, i].astype(F32).T

        @pl.loop(0, in_chunk // step)
        def _(i):
            gs = [c * in_chunk + i * step + u for u in range(step)]
            a = [first(g) for g in gs]
            m = [second(g, r[7], r[8]) for g, r in zip(gs, a)]
            for g, r, z in zip(gs, a, m):
                third(g, *r[:7], *z)

        for i in range(n_ctx):
            blk_s[c, i] = blk_t[cs, i * own_len:(i + 1) * own_len].T.astype(BF16)
            gin_s[c, i] = gin_t[cs, i * own_len:(i + 1) * own_len].T.astype(BF16)
        for k in range(1, n_ctx):
            for copy in results(c, k):
                copy.start()
        for copy in own_results(c):
            copy.start()

    t = 0
    for r in range(groups // 8):
        for i in range(n):
            red[t] = long_s[r * 8:(r + 1) * 8, i * LANES:(i + 1) * LANES]
            t += 1
    for c in range(chunks):
        turned = short_t[c * LANES:(c + 1) * LANES, :].T
        for r in range(3):
            red[t] = turned[r * 8:(r + 1) * 8, :]
            t += 1

    def part_copy(k, slot):
        return remote(red.at[pl.ds(dp(k) * per, per)], got.at[slot],
                      red_send.at[k], red_recv.at[k], {"dp": dp(k)})

    def sum_copy(k, slot):
        return remote(summed.at[mine], summed.at[slot],
                      sum_send.at[k], sum_recv.at[k], {"dp": dp(k)})

    for k in range(1, n_dp):
        part_copy(k, mine).start()
    got[mine] = red[pl.ds(mine * per, per)]
    for k in range(1, n_dp):
        part_copy(k, dp(n_dp - k)).wait()
    total = got[0]
    for i in range(1, n_dp):
        total = total + got[i]
    summed[mine] = total
    for k in range(1, n_dp):
        sum_copy(k, mine).start()
    for k in range(1, n_dp):
        sum_copy(k, dp(n_dp - k)).wait()

    base_t = (groups // 8) * n
    for c in range(chunks):
        for r in range(3):
            t = base_t + c * 3 + r
            short_b[me, r, :, c * LANES:(c + 1) * LANES] = summed[t // per, t % per]

    def short_copy(k, slot):
        return remote(short_b.at[me], short_b.at[slot],
                      sh_send.at[k], sh_recv.at[k], {"ctx": ctx(k)})

    for k in range(1, n_ctx):
        short_copy(k, me).start()
    t = 0
    for r in range(groups // 8):
        for i in range(n):
            long_ref[r * 8:(r + 1) * 8, i * LANES:(i + 1) * LANES] = summed[t // per, t % per]
            t += 1
    for k in range(1, n_ctx):
        short_copy(k, ctx(n_ctx - k)).wait()
    for i in range(n_ctx):
        for s in range(3):
            short_ref[s, :, i * chans:(i + 1) * chans] = short_b[i, s, :taps, :]

    @pl.loop(0, chunks)
    def _(c):
        for k in range(1, n_ctx):
            for copy in arrivals(c, k):
                copy.wait()
        for copy in own_results(c):
            copy.wait()


def on_device(tokens, embedding, cotangent, long_filter, short_filter):
    streams, taps, channels = short_filter.shape
    vocab = embedding.shape[0]
    n_ctx = lax.axis_size("ctx")
    n_dp = lax.axis_size("dp")
    chans = channels // n_ctx
    groups, length = long_filter.shape
    own_len = cotangent.shape[1]
    chunks = chans // LANES
    tiles = (groups // 8) * (length // LANES) + streams * chunks
    per = -(-tiles // n_dp)
    vmem = pl.BlockSpec(memory_space=pltpu.VMEM)
    hbm = pl.BlockSpec(memory_space=pl.ANY)
    dma = pltpu.SemaphoreType.DMA
    return pl.pallas_call(
        kernel,
        out_shape=[
            jax.ShapeDtypeStruct(cotangent.shape, BF16),
            jax.ShapeDtypeStruct(cotangent.shape, BF16),
            jax.ShapeDtypeStruct((groups, length), F32),
            jax.ShapeDtypeStruct(short_filter.shape, F32),
        ],
        in_specs=[vmem, hbm, hbm, vmem, vmem],
        out_specs=[hbm, hbm, vmem, vmem],
        scratch_shapes=[
            pltpu.VMEM((n_ctx, 1, own_len), jnp.int32),
            pltpu.VMEM((vocab, chans), BF16),
            pltpu.VMEM((chunks, n_ctx, own_len, LANES), BF16),
            pltpu.VMEM((vocab, length), BF16),
            pltpu.VMEM((chans, length), F32),
            pltpu.VMEM((chans, length), F32),
            pltpu.VMEM((chans, length), F32),
            pltpu.VMEM((chans, length), F32),
            pltpu.VMEM((LANES, chans), F32),
            pltpu.VMEM((chans, LANES), F32),
            pltpu.VMEM((chunks, n_ctx, own_len, LANES), BF16),
            pltpu.VMEM((chunks, n_ctx, own_len, LANES), BF16),
            pltpu.VMEM((groups, length), F32),
            pltpu.VMEM((chans, LANES), F32),
            pltpu.VMEM((per * n_dp, 8, LANES), F32),
            pltpu.VMEM((n_dp, per, 8, LANES), F32),
            pltpu.VMEM((n_dp, per, 8, LANES), F32),
            pltpu.VMEM((n_ctx, streams, 8, chans), F32),
            dma, dma((chunks,)), dma((2, chunks)),
            dma((n_ctx,)), dma((n_ctx,)),
            dma((chunks, n_ctx)), dma((chunks, n_ctx)),
            dma((2, chunks, n_ctx)), dma((2, chunks, n_ctx)),
            dma((n_dp,)), dma((n_dp,)), dma((n_dp,)), dma((n_dp,)),
            dma((n_ctx,)), dma((n_ctx,)),
        ],
        compiler_params=pltpu.CompilerParams(
            vmem_limit_bytes=48 * 1024 * 1024, collective_id=0, has_side_effects=True),
        name="hyena",
    )(tokens, embedding, cotangent, long_filter, short_filter)


def solution(mesh):
    in_specs = (P("dp", "ctx"), P(), P("dp", "ctx", None), P("ctx", None), P())
    out_specs = (P("dp", "ctx", None), P("dp", "ctx", None), P("ctx", None), P())
    return jax.shard_map(
        on_device, mesh=mesh, in_specs=in_specs, out_specs=out_specs, check_vma=False
    )
```

```python
import jax
import jax.numpy as jnp
from jax import lax
from jax.experimental import pallas as pl
from jax.experimental.pallas import tpu as pltpu
from jax.sharding import PartitionSpec as P

LANES = 128
VMEM_LIMIT = 63 * 1024 * 1024
F32 = jnp.float32
BF16 = jnp.bfloat16
MESH = pl.DeviceIdType.MESH


def contract(a, b, da, db):
    return lax.dot_general(a, b, (((da,), (db,)), ((), ())), preferred_element_type=F32)


def kernel(tok_ref, emb_ref, cot_ref, h_in, w_in,
           blk_ref, gin_ref, long_ref, short_ref,
           ids, emb, cot_b, hot, e_t, cot_t, blk_t, gin_t, w_s, w_t, blk_s, gin_s,
           long_s, short_t, red, got, summed, short_b, h_ref, w_ref,
           emb_sem, in_sem, own_sem, out_sem, tok_send, tok_recv, cot_send, cot_recv,
           res_send, res_recv, red_send, red_recv, sum_send, sum_recv, sh_send, sh_recv):
    n_ctx, n_dp = lax.axis_size("ctx"), lax.axis_size("dp")
    me, mine = lax.axis_index("ctx"), lax.axis_index("dp")
    vocab, chans = emb.shape
    taps = w_ref.shape[1]
    groups, length = h_ref.shape
    group = chans // groups
    n = length // LANES
    own_len = tok_ref.shape[1]
    chunks = chans // LANES
    scale = 1.0 / (n_dp * group)
    per = got.shape[2]
    where = pl.ds(pl.multiple_of(me * chans, chans), chans)

    def ctx(k):
        return lax.rem(me + k, n_ctx)

    def dp(k):
        return lax.rem(mine + k, n_dp)

    def remote(src, dst, send, recv, target):
        return pltpu.make_async_remote_copy(
            src_ref=src, dst_ref=dst, send_sem=send, recv_sem=recv,
            device_id=target, device_id_type=MESH)

    emb_copy = pltpu.make_async_copy(emb_ref.at[:, where], emb, emb_sem)
    emb_copy.start()
    loads = [pltpu.make_async_copy(h_in, h_ref, in_sem.at[0]),
             pltpu.make_async_copy(w_in.at[:, :, where], w_ref, in_sem.at[1]),
             pltpu.make_async_copy(tok_ref, ids.at[me], in_sem.at[2])]
    for copy in loads:
        copy.start()

    def cot_part(p, c):
        return cot_ref.at[0, :, pl.ds(pl.multiple_of(p * chans + c * LANES, LANES), LANES)]

    def own_cot(c):
        return pltpu.make_async_copy(cot_part(me, c), cot_b.at[c, me], own_sem.at[c])

    for c in range(chunks):
        own_cot(c).start()

    barrier = pltpu.get_barrier_semaphore()
    for k in range(1, n_ctx):
        pl.semaphore_signal(barrier, inc=1, device_id={"ctx": ctx(k)}, device_id_type=MESH)

    @pl.loop(1, n_dp)
    def _(k):
        pl.semaphore_signal(barrier, inc=1, device_id={"dp": dp(k)}, device_id_type=MESH)

    pl.semaphore_wait(barrier, n_ctx + n_dp - 2)

    def tok_copy(k, slot):
        return remote(tok_ref, ids.at[slot], tok_send.at[k], tok_recv.at[k], {"ctx": ctx(k)})

    def cot_copy(k, c, slot):
        return remote(cot_part(ctx(k), c), cot_b.at[c, slot],
                      cot_send.at[c, k], cot_recv.at[c, k], {"ctx": ctx(k)})

    for k in range(1, n_ctx):
        tok_copy(k, me).start()
    for c in range(chunks):
        for k in range(1, n_ctx):
            cot_copy(k, c, me).start()
    for copy in loads:
        copy.wait()

    w_s[...] = jnp.zeros_like(w_s)
    for s in range(3):
        w_s[s * 8:s * 8 + taps, :] = w_ref[s, :, :]
    for c in range(chunks):
        w_t[c * LANES:(c + 1) * LANES, :] = w_s[:, c * LANES:(c + 1) * LANES].T
    if red.shape[1] > n + 3:
        red[...] = jnp.zeros_like(red)

    for k in range(1, n_ctx):
        tok_copy(k, ctx(n_ctx - k)).wait()
    rows_v = lax.broadcasted_iota(jnp.int32, (vocab, own_len), 0)
    for i in range(n_ctx):
        hot[:, i * own_len:(i + 1) * own_len] = (rows_v == ids[i]).astype(F32).astype(BF16)
    emb_copy.wait()

    sub_i = lax.broadcasted_iota(jnp.int32, (LANES, LANES), 0)
    lane_i = lax.broadcasted_iota(jnp.int32, (LANES, LANES), 1)
    upper = lane_i >= sub_i
    lane = lax.broadcasted_iota(jnp.int32, (group, length), 1)
    lane_k = lax.broadcasted_iota(jnp.int32, (group, LANES), 1)

    def first(g):
        rows = pl.ds(pl.multiple_of(g * group, group), group)
        e = e_t[rows, :]
        es = [e] + [jnp.where(lane >= j, pltpu.roll(e, j, 1), 0.0) for j in range(1, taps)]
        w = w_t[rows, :]
        col = [[w[:, s * 8 + j:s * 8 + j + 1] for j in range(taps)] for s in range(3)]

        def stream(s):
            total = col[s][0] * es[0]
            for j in range(1, taps):
                total = total + col[s][j] * es[j]
            return total

        q, k, v = stream(0), stream(1), stream(2)
        cot = cot_t[rows, :]
        x = (k * v).astype(BF16)
        gc = (cot * q).astype(BF16)
        return rows, es, col, q, k, v, cot, x, gc

    def second(g, x, gc):
        xb = [x[:, i * LANES:(i + 1) * LANES] for i in range(n)]
        gb = [gc[:, i * LANES:(i + 1) * LANES] for i in range(n)]
        zero = jnp.zeros((group, LANES), BF16)
        lx = jnp.concatenate(
            [jnp.concatenate([xb[i - d] if d <= i else zero for d in range(n)], axis=1)
             for i in range(n)], axis=0)
        lg = jnp.concatenate(
            [jnp.concatenate([gb[i + d] if i + d < n else zero for d in range(n)], axis=1)
             for i in range(n)], axis=0)
        xs = jnp.concatenate(xb, axis=0)
        h = h_ref[pl.ds(g, 1), :]
        prev = jnp.zeros((LANES, LANES), F32)
        ws = []
        for d in range(n):
            part = jnp.broadcast_to(h[:, d * LANES:(d + 1) * LANES], (8, LANES))
            base = pltpu.roll(part, 0, 1, stride=1, stride_axis=0)
            turned = jnp.concatenate(
                [base] + [pltpu.roll(base, m, 1) for m in range(8, LANES, 8)], axis=0)
            ws.append(jnp.where(upper, turned, prev).astype(BF16))
            prev = turned
        conv = contract(lx, jnp.concatenate(ws, axis=0), 1, 0)
        gg = contract(lg, jnp.concatenate(ws, axis=1), 1, 1)
        cross = contract(xs, lg, 0, 0)
        return conv, gg, cross

    def wide(a):
        return jnp.concatenate([a[i * group:(i + 1) * group] for i in range(n)], axis=1)

    def third(g, rows, es, col, q, k, v, cot, conv, gg, cross):
        cross = jnp.concatenate(
            [jnp.where(upper, cross[:, :LANES], 0.0), cross[:, LANES:]], axis=1)
        size = LANES
        while size > 8:
            size //= 2
            cross = cross[:size] + pltpu.roll(cross[size:], length - size, 1)
        while size > 1:
            size //= 2
            cross = cross + pltpu.roll(pltpu.roll(cross, 8 - size, 0), length - size, 1)
        long_s[pl.ds(g, 1), :] = cross[0:1] * scale

        cb = wide(conv).astype(BF16).astype(F32)
        gb2 = wide(gg).astype(BF16).astype(F32)
        blk_t[rows, :] = q * cb
        grads = [cot * cb, gb2 * v, gb2 * k]
        total = None
        for j in range(taps - 1, -1, -1):
            term = col[0][j] * grads[0] + col[1][j] * grads[1] + col[2][j] * grads[2]
            if total is not None:
                term = term + jnp.where(lane < length - 1, pltpu.roll(total, length - 1, 1), 0.0)
            total = term
        gin_t[rows, :] = total
        acc = jnp.zeros((group, LANES), F32)
        for s in range(3):
            for j in range(taps):
                prod = grads[s] * es[j]
                fold = prod[:, :LANES]
                for i in range(1, n):
                    fold = fold + prod[:, i * LANES:(i + 1) * LANES]
                acc = jnp.where(lane_k == s * 8 + j, jnp.sum(fold, axis=1, keepdims=True), acc)
        short_t[rows, :] = acc * scale

    def results(c, k):
        at = pl.ds(pl.multiple_of(me * chans + c * LANES, LANES), LANES)
        to = ctx(k)
        return [remote(src.at[c, to], dst.at[0, :, at], res_send.at[i, c, k],
                       res_recv.at[i, c, k], {"ctx": to})
                for i, (src, dst) in enumerate(((blk_s, blk_ref), (gin_s, gin_ref)))]

    def arrivals(c, k):
        src_dev = ctx(n_ctx - k)
        at = pl.ds(pl.multiple_of(src_dev * chans + c * LANES, LANES), LANES)
        return [remote(src.at[c, me], dst.at[0, :, at], res_send.at[i, c, k],
                       res_recv.at[i, c, k], {"ctx": ctx(k)})
                for i, (src, dst) in enumerate(((blk_s, blk_ref), (gin_s, gin_ref)))]

    def own_results(c):
        at = pl.ds(pl.multiple_of(me * chans + c * LANES, LANES), LANES)
        return [pltpu.make_async_copy(src.at[c, me], dst.at[0, :, at], out_sem.at[i, c])
                for i, (src, dst) in enumerate(((blk_s, blk_ref), (gin_s, gin_ref)))]

    def part_copy(c, k, slot):
        return remote(red.at[c, pl.ds(dp(k) * per, per)], got.at[c, slot],
                      red_send.at[c, k], red_recv.at[c, k], {"dp": dp(k)})

    def sum_copy(c, k, slot):
        return remote(summed.at[c, mine], summed.at[c, slot],
                      sum_send.at[c, k], sum_recv.at[c, k], {"dp": dp(k)})

    def short_copy(c, k, slot):
        return remote(short_b.at[c, me], short_b.at[c, slot],
                      sh_send.at[c, k], sh_recv.at[c, k], {"ctx": ctx(k)})

    def scatter(c):
        cs = pl.ds(pl.multiple_of(c * LANES, LANES), LANES)
        gs = pl.ds(pl.multiple_of(c * in_chunk, in_chunk), in_chunk)
        for i in range(n):
            red[c, i] = long_s[gs, i * LANES:(i + 1) * LANES]
        turned = short_t[cs, :].T
        for r in range(3):
            red[c, n + r] = turned[r * 8:(r + 1) * 8, :]
        for k in range(1, n_dp):
            part_copy(c, k, mine).start()
        got[c, mine] = red[c, pl.ds(mine * per, per)]

    def reduce(c):
        for k in range(1, n_dp):
            part_copy(c, k, dp(n_dp - k)).wait()
        total = got[c, 0]
        for i in range(1, n_dp):
            total = total + got[c, i]
        summed[c, mine] = total
        for k in range(1, n_dp):
            sum_copy(c, k, mine).start()

    def finish(c):
        for k in range(1, n_dp):
            sum_copy(c, k, dp(n_dp - k)).wait()
        for r in range(3):
            short_b[c, me, r] = summed[c, (n + r) // per, (n + r) % per]
        for k in range(1, n_ctx):
            short_copy(c, k, me).start()

    in_chunk = LANES // group
    step = 2 if in_chunk % 2 == 0 else 1

    @pl.loop(0, chunks)
    def _(c):
        cs = pl.ds(pl.multiple_of(c * LANES, LANES), LANES)
        e_t[cs, :] = contract(emb[:, cs], hot[...], 0, 0)
        own_cot(c).wait()
        for k in range(1, n_ctx):
            cot_copy(k, c, ctx(n_ctx - k)).wait()
        for i in range(n_ctx):
            cot_t[cs, i * own_len:(i + 1) * own_len] = cot_b[c, i].astype(F32).T

        @pl.loop(0, in_chunk // step)
        def _(i):
            gs = [c * in_chunk + i * step + u for u in range(step)]
            a = [first(g) for g in gs]
            m = [second(g, r[7], r[8]) for g, r in zip(gs, a)]
            for g, r, z in zip(gs, a, m):
                third(g, *r[:7], *z)

        scatter(c)
        for i in range(n_ctx):
            blk_s[c, i] = blk_t[cs, i * own_len:(i + 1) * own_len].T.astype(BF16)
            gin_s[c, i] = gin_t[cs, i * own_len:(i + 1) * own_len].T.astype(BF16)
        for k in range(1, n_ctx):
            for copy in results(c, k):
                copy.start()
        for copy in own_results(c):
            copy.start()

        @pl.when(c > 0)
        def _():
            reduce(c - 1)

        @pl.when(c > 1)
        def _():
            finish(c - 2)

    reduce(chunks - 1)
    for c in range(max(chunks - 2, 0), chunks):
        finish(c)
    for c in range(chunks):
        for i in range(n):
            long_ref[c * in_chunk:(c + 1) * in_chunk, i * LANES:(i + 1) * LANES] = (
                summed[c, i // per, i % per])
    for c in range(chunks):
        for k in range(1, n_ctx):
            short_copy(c, k, ctx(n_ctx - k)).wait()
        for i in range(n_ctx):
            for s in range(3):
                at = i * chans + c * LANES
                short_ref[s, :, at:at + LANES] = short_b[c, i, s, :taps, :]

    @pl.loop(0, chunks)
    def _(c):
        for k in range(1, n_ctx):
            for copy in arrivals(c, k):
                copy.wait()
        for copy in own_results(c):
            copy.wait()


def hand_over(*refs):
    sems = refs[8]
    copies = [pltpu.make_async_copy(refs[i], refs[4 + i], sems.at[i]) for i in range(4)]
    for copy in copies:
        copy.start()
    for copy in copies:
        copy.wait()


def on_device(tokens, embedding, cotangent, long_filter, short_filter):
    streams, taps, channels = short_filter.shape
    vocab = embedding.shape[0]
    n_ctx = lax.axis_size("ctx")
    n_dp = lax.axis_size("dp")
    chans = channels // n_ctx
    groups, length = long_filter.shape
    own_len = cotangent.shape[1]
    chunks = chans // LANES
    per = -(-(length // LANES + streams) // n_dp)
    vmem = pl.BlockSpec(memory_space=pltpu.VMEM)
    hbm = pl.BlockSpec(memory_space=pltpu.HBM)
    dma = pltpu.SemaphoreType.DMA
    parts = pl.pallas_call(
        kernel,
        out_shape=[
            jax.ShapeDtypeStruct(cotangent.shape, BF16),
            jax.ShapeDtypeStruct(cotangent.shape, BF16),
            jax.ShapeDtypeStruct((groups, length), F32),
            jax.ShapeDtypeStruct(short_filter.shape, F32),
        ],
        in_specs=[hbm] * 5,
        out_specs=[hbm, hbm, vmem, vmem],
        scratch_shapes=[
            pltpu.VMEM((n_ctx, 1, own_len), jnp.int32),
            pltpu.VMEM((vocab, chans), BF16),
            pltpu.VMEM((chunks, n_ctx, own_len, LANES), BF16),
            pltpu.VMEM((vocab, length), BF16),
            pltpu.VMEM((chans, length), F32),
            pltpu.VMEM((chans, length), F32),
            pltpu.VMEM((chans, length), F32),
            pltpu.VMEM((chans, length), F32),
            pltpu.VMEM((LANES, chans), F32),
            pltpu.VMEM((chans, LANES), F32),
            pltpu.VMEM((chunks, n_ctx, own_len, LANES), BF16),
            pltpu.VMEM((chunks, n_ctx, own_len, LANES), BF16),
            pltpu.VMEM((groups, length), F32),
            pltpu.VMEM((chans, LANES), F32),
            pltpu.VMEM((chunks, per * n_dp, 8, LANES), F32),
            pltpu.VMEM((chunks, n_dp, per, 8, LANES), F32),
            pltpu.VMEM((chunks, n_dp, per, 8, LANES), F32),
            pltpu.VMEM((chunks, n_ctx, streams, 8, LANES), F32),
            pltpu.VMEM((groups, length), F32),
            pltpu.VMEM((streams, taps, chans), F32),
            dma, dma((3,)), dma((chunks,)), dma((2, chunks)),
            dma((n_ctx,)), dma((n_ctx,)),
            dma((chunks, n_ctx)), dma((chunks, n_ctx)),
            dma((2, chunks, n_ctx)), dma((2, chunks, n_ctx)),
            dma((chunks, n_dp)), dma((chunks, n_dp)), dma((chunks, n_dp)), dma((chunks, n_dp)),
            dma((chunks, n_ctx)), dma((chunks, n_ctx)),
        ],
        compiler_params=pltpu.CompilerParams(
            vmem_limit_bytes=VMEM_LIMIT, collective_id=0, has_side_effects=True),
        name="hyena",
    )(tokens, embedding, cotangent, long_filter, short_filter)
    anywhere = pl.BlockSpec(memory_space=pl.ANY)
    return pl.pallas_call(
        hand_over,
        out_shape=[jax.ShapeDtypeStruct(p.shape, p.dtype) for p in parts],
        in_specs=[anywhere] * 4,
        out_specs=[anywhere] * 4,
        scratch_shapes=[dma((4,))],
        compiler_params=pltpu.CompilerParams(vmem_limit_bytes=VMEM_LIMIT),
        name="hand_over",
    )(*parts)


def solution(mesh):
    in_specs = (P("dp", "ctx"), P(), P("dp", "ctx", None), P("ctx", None), P())
    out_specs = (P("dp", "ctx", None), P("dp", "ctx", None), P("ctx", None), P())
    return jax.shard_map(
        on_device, mesh=mesh, in_specs=in_specs, out_specs=out_specs, check_vma=False
    )
```

```python
import jax
import jax.numpy as jnp
from jax import lax
from jax.experimental import pallas as pl
from jax.experimental.pallas import tpu as pltpu
from jax.sharding import PartitionSpec as P

LANES = 128
VMEM_LIMIT = 63 * 1024 * 1024
F32 = jnp.float32
BF16 = jnp.bfloat16
MESH = pl.DeviceIdType.MESH


def contract(a, b, da, db):
    return lax.dot_general(a, b, (((da,), (db,)), ((), ())), preferred_element_type=F32)


def kernel(tok_ref, emb_ref, cot_ref, h_in, w_in,
           blk_ref, gin_ref, long_ref, short_ref,
           ids, emb, cot_b, hot, e_t, cot_t, blk_t, gin_t, w_s, w_t, blk_s, gin_s,
           long_s, short_t, red, got, summed, short_b, h_ref, w_ref,
           emb_sem, in_sem, own_sem, out_sem, tok_send, tok_recv, cot_send, cot_recv,
           res_send, res_recv, red_send, red_recv, sum_send, sum_recv, sh_send, sh_recv):
    n_ctx, n_dp = lax.axis_size("ctx"), lax.axis_size("dp")
    me, mine = lax.axis_index("ctx"), lax.axis_index("dp")
    vocab, chans = emb.shape
    taps = w_ref.shape[1]
    groups, length = h_ref.shape
    group = chans // groups
    n = length // LANES
    own_len = tok_ref.shape[1]
    chunks = chans // LANES
    scale = 1.0 / (n_dp * group)
    per = got.shape[2]
    where = pl.ds(pl.multiple_of(me * chans, chans), chans)

    def ctx(k):
        return lax.rem(me + k, n_ctx)

    def dp(k):
        return lax.rem(mine + k, n_dp)

    def remote(src, dst, send, recv, target):
        return pltpu.make_async_remote_copy(
            src_ref=src, dst_ref=dst, send_sem=send, recv_sem=recv,
            device_id=target, device_id_type=MESH)

    emb_copy = pltpu.make_async_copy(emb_ref.at[:, where], emb, emb_sem)
    emb_copy.start()
    loads = [pltpu.make_async_copy(h_in, h_ref, in_sem.at[0]),
             pltpu.make_async_copy(w_in.at[:, :, where], w_ref, in_sem.at[1]),
             pltpu.make_async_copy(tok_ref, ids.at[me], in_sem.at[2])]
    for copy in loads:
        copy.start()

    def cot_part(p, c):
        return cot_ref.at[0, :, pl.ds(pl.multiple_of(p * chans + c * LANES, LANES), LANES)]

    def own_cot(c):
        return pltpu.make_async_copy(cot_part(me, c), cot_b.at[c, me], own_sem.at[c])

    for c in range(chunks):
        own_cot(c).start()

    barrier = pltpu.get_barrier_semaphore()
    for k in range(1, n_ctx):
        pl.semaphore_signal(barrier, inc=1, device_id={"ctx": ctx(k)}, device_id_type=MESH)

    @pl.loop(1, n_dp)
    def _(k):
        pl.semaphore_signal(barrier, inc=1, device_id={"dp": dp(k)}, device_id_type=MESH)

    pl.semaphore_wait(barrier, n_ctx + n_dp - 2)

    def tok_copy(k, slot):
        return remote(tok_ref, ids.at[slot], tok_send.at[k], tok_recv.at[k], {"ctx": ctx(k)})

    def cot_copy(k, c, slot):
        return remote(cot_part(ctx(k), c), cot_b.at[c, slot],
                      cot_send.at[c, k], cot_recv.at[c, k], {"ctx": ctx(k)})

    for k in range(1, n_ctx):
        tok_copy(k, me).start()
    for c in range(chunks):
        for k in range(1, n_ctx):
            cot_copy(k, c, me).start()
    for copy in loads:
        copy.wait()

    w_s[...] = jnp.zeros_like(w_s)
    for s in range(3):
        w_s[s * 8:s * 8 + taps, :] = w_ref[s, :, :]
    for c in range(chunks):
        w_t[c * LANES:(c + 1) * LANES, :] = w_s[:, c * LANES:(c + 1) * LANES].T
    if red.shape[1] > n + 3:
        red[...] = jnp.zeros_like(red)

    for k in range(1, n_ctx):
        tok_copy(k, ctx(n_ctx - k)).wait()
    rows_v = lax.broadcasted_iota(jnp.int32, (vocab, own_len), 0)
    for i in range(n_ctx):
        hot[:, i * own_len:(i + 1) * own_len] = (rows_v == ids[i]).astype(F32).astype(BF16)
    emb_copy.wait()

    sub_i = lax.broadcasted_iota(jnp.int32, (LANES, LANES), 0)
    lane_i = lax.broadcasted_iota(jnp.int32, (LANES, LANES), 1)
    upper = lane_i >= sub_i
    lane = lax.broadcasted_iota(jnp.int32, (group, length), 1)
    lane_k = lax.broadcasted_iota(jnp.int32, (group, LANES), 1)

    def first(g):
        rows = pl.ds(pl.multiple_of(g * group, group), group)
        e = e_t[rows, :]
        es = [e] + [jnp.where(lane >= j, pltpu.roll(e, j, 1), 0.0) for j in range(1, taps)]
        w = w_t[rows, :]
        col = [[w[:, s * 8 + j:s * 8 + j + 1] for j in range(taps)] for s in range(3)]

        def stream(s):
            total = col[s][0] * es[0]
            for j in range(1, taps):
                total = total + col[s][j] * es[j]
            return total

        q, k, v = stream(0), stream(1), stream(2)
        cot = cot_t[rows, :]
        x = (k * v).astype(BF16)
        gc = (cot * q).astype(BF16)
        return rows, es, col, q, k, v, cot, x, gc

    def second(g, x, gc):
        xb = [x[:, i * LANES:(i + 1) * LANES] for i in range(n)]
        gb = [gc[:, i * LANES:(i + 1) * LANES] for i in range(n)]
        zero = jnp.zeros((group, LANES), BF16)
        lx = jnp.concatenate(
            [jnp.concatenate([xb[i - d] if d <= i else zero for d in range(n)], axis=1)
             for i in range(n)], axis=0)
        lg = jnp.concatenate(
            [jnp.concatenate([gb[i + d] if i + d < n else zero for d in range(n)], axis=1)
             for i in range(n)], axis=0)
        xs = jnp.concatenate(xb, axis=0)
        h = h_ref[pl.ds(g, 1), :]
        prev = jnp.zeros((LANES, LANES), F32)
        ws = []
        for d in range(n):
            part = jnp.broadcast_to(h[:, d * LANES:(d + 1) * LANES], (8, LANES))
            base = pltpu.roll(part, 0, 1, stride=1, stride_axis=0)
            turned = jnp.concatenate(
                [base] + [pltpu.roll(base, m, 1) for m in range(8, LANES, 8)], axis=0)
            ws.append(jnp.where(upper, turned, prev).astype(BF16))
            prev = turned
        conv = contract(lx, jnp.concatenate(ws, axis=0), 1, 0)
        gg = contract(lg, jnp.concatenate(ws, axis=1), 1, 1)
        cross = contract(xs, lg, 0, 0)
        return conv, gg, cross

    def wide(a):
        return jnp.concatenate([a[i * group:(i + 1) * group] for i in range(n)], axis=1)

    def third(g, rows, es, col, q, k, v, cot, conv, gg, cross):
        cross = jnp.concatenate(
            [jnp.where(upper, cross[:, :LANES], 0.0), cross[:, LANES:]], axis=1)
        size = LANES
        while size > 8:
            size //= 2
            cross = cross[:size] + pltpu.roll(cross[size:], length - size, 1)
        while size > 1:
            size //= 2
            cross = cross + pltpu.roll(pltpu.roll(cross, 8 - size, 0), length - size, 1)
        long_s[pl.ds(g, 1), :] = cross[0:1] * scale

        cb = wide(conv).astype(BF16).astype(F32)
        gb2 = wide(gg).astype(BF16).astype(F32)
        blk_t[rows, :] = q * cb
        grads = [cot * cb, gb2 * v, gb2 * k]
        total = None
        for j in range(taps - 1, -1, -1):
            term = col[0][j] * grads[0] + col[1][j] * grads[1] + col[2][j] * grads[2]
            if total is not None:
                term = term + jnp.where(lane < length - 1, pltpu.roll(total, length - 1, 1), 0.0)
            total = term
        gin_t[rows, :] = total
        acc = jnp.zeros((group, LANES), F32)
        for s in range(3):
            for j in range(taps):
                prod = grads[s] * es[j]
                fold = prod[:, :LANES]
                for i in range(1, n):
                    fold = fold + prod[:, i * LANES:(i + 1) * LANES]
                acc = jnp.where(lane_k == s * 8 + j, jnp.sum(fold, axis=1, keepdims=True), acc)
        short_t[rows, :] = acc * scale

    def results(c, k):
        at = pl.ds(pl.multiple_of(me * chans + c * LANES, LANES), LANES)
        to = ctx(k)
        return [remote(src.at[c, to], dst.at[0, :, at], res_send.at[i, c, k],
                       res_recv.at[i, c, k], {"ctx": to})
                for i, (src, dst) in enumerate(((blk_s, blk_ref), (gin_s, gin_ref)))]

    def arrivals(c, k):
        src_dev = ctx(n_ctx - k)
        at = pl.ds(pl.multiple_of(src_dev * chans + c * LANES, LANES), LANES)
        return [remote(src.at[c, me], dst.at[0, :, at], res_send.at[i, c, k],
                       res_recv.at[i, c, k], {"ctx": ctx(k)})
                for i, (src, dst) in enumerate(((blk_s, blk_ref), (gin_s, gin_ref)))]

    def own_results(c):
        at = pl.ds(pl.multiple_of(me * chans + c * LANES, LANES), LANES)
        return [pltpu.make_async_copy(src.at[c, me], dst.at[0, :, at], out_sem.at[i, c])
                for i, (src, dst) in enumerate(((blk_s, blk_ref), (gin_s, gin_ref)))]

    def part_copy(c, k, slot):
        return remote(red.at[c, pl.ds(dp(k) * per, per)], got.at[c, slot],
                      red_send.at[c, k], red_recv.at[c, k], {"dp": dp(k)})

    def sum_copy(c, k, slot):
        return remote(summed.at[c, mine], summed.at[c, slot],
                      sum_send.at[c, k], sum_recv.at[c, k], {"dp": dp(k)})

    def short_copy(c, k, slot):
        return remote(short_b.at[c, me], short_b.at[c, slot],
                      sh_send.at[c, k], sh_recv.at[c, k], {"ctx": ctx(k)})

    def scatter(c):
        cs = pl.ds(pl.multiple_of(c * LANES, LANES), LANES)
        gs = pl.ds(pl.multiple_of(c * in_chunk, in_chunk), in_chunk)
        for i in range(n):
            red[c, i] = long_s[gs, i * LANES:(i + 1) * LANES]
        turned = short_t[cs, :].T
        for r in range(3):
            red[c, n + r] = turned[r * 8:(r + 1) * 8, :]
        for k in range(1, n_dp):
            part_copy(c, k, mine).start()
        got[c, mine] = red[c, pl.ds(mine * per, per)]

    def reduce(c):
        for k in range(1, n_dp):
            part_copy(c, k, dp(n_dp - k)).wait()
        total = got[c, 0]
        for i in range(1, n_dp):
            total = total + got[c, i]
        summed[c, mine] = total
        for k in range(1, n_dp):
            sum_copy(c, k, mine).start()

    def finish(c):
        for k in range(1, n_dp):
            sum_copy(c, k, dp(n_dp - k)).wait()
        for r in range(3):
            short_b[c, me, r] = summed[c, (n + r) // per, (n + r) % per]
        for k in range(1, n_ctx):
            short_copy(c, k, me).start()

    in_chunk = LANES // group
    step = 2 if in_chunk % 2 == 0 else 1

    @pl.loop(0, chunks)
    def _(c):
        cs = pl.ds(pl.multiple_of(c * LANES, LANES), LANES)
        e_t[cs, :] = contract(emb[:, cs], hot[...], 0, 0)
        own_cot(c).wait()
        for k in range(1, n_ctx):
            cot_copy(k, c, ctx(n_ctx - k)).wait()
        for i in range(n_ctx):
            cot_t[cs, i * own_len:(i + 1) * own_len] = cot_b[c, i].astype(F32).T

        @pl.loop(0, in_chunk // step)
        def _(i):
            gs = [c * in_chunk + i * step + u for u in range(step)]
            a = [first(g) for g in gs]
            m = [second(g, r[7], r[8]) for g, r in zip(gs, a)]
            for g, r, z in zip(gs, a, m):
                third(g, *r[:7], *z)

        scatter(c)
        for i in range(n_ctx):
            blk_s[c, i] = blk_t[cs, i * own_len:(i + 1) * own_len].T.astype(BF16)
            gin_s[c, i] = gin_t[cs, i * own_len:(i + 1) * own_len].T.astype(BF16)
        for k in range(1, n_ctx):
            for copy in results(c, k):
                copy.start()
        for copy in own_results(c):
            copy.start()

        @pl.when(c > 0)
        def _():
            reduce(c - 1)

        @pl.when(c > 1)
        def _():
            finish(c - 2)

    reduce(chunks - 1)
    for c in range(max(chunks - 2, 0), chunks):
        finish(c)
    for c in range(chunks):
        for i in range(n):
            long_ref[c * in_chunk:(c + 1) * in_chunk, i * LANES:(i + 1) * LANES] = (
                summed[c, i // per, i % per])
    for c in range(chunks):
        for k in range(1, n_ctx):
            short_copy(c, k, ctx(n_ctx - k)).wait()
        for i in range(n_ctx):
            for s in range(3):
                at = i * chans + c * LANES
                short_ref[s, :, at:at + LANES] = short_b[c, i, s, :taps, :]

    @pl.loop(0, chunks)
    def _(c):
        for k in range(1, n_ctx):
            for copy in arrivals(c, k):
                copy.wait()
        for copy in own_results(c):
            copy.wait()


def on_device(tokens, embedding, cotangent, long_filter, short_filter):
    streams, taps, channels = short_filter.shape
    vocab = embedding.shape[0]
    n_ctx = lax.axis_size("ctx")
    n_dp = lax.axis_size("dp")
    chans = channels // n_ctx
    groups, length = long_filter.shape
    own_len = cotangent.shape[1]
    chunks = chans // LANES
    per = -(-(length // LANES + streams) // n_dp)
    vmem = pl.BlockSpec(memory_space=pltpu.VMEM)
    hbm = pl.BlockSpec(memory_space=pltpu.HBM)
    dma = pltpu.SemaphoreType.DMA
    parts = pl.pallas_call(
        kernel,
        out_shape=[
            jax.ShapeDtypeStruct(cotangent.shape, BF16),
            jax.ShapeDtypeStruct(cotangent.shape, BF16),
            jax.ShapeDtypeStruct((groups, length), F32),
            jax.ShapeDtypeStruct(short_filter.shape, F32),
        ],
        in_specs=[hbm] * 5,
        out_specs=[hbm, hbm, vmem, vmem],
        scratch_shapes=[
            pltpu.VMEM((n_ctx, 1, own_len), jnp.int32),
            pltpu.VMEM((vocab, chans), BF16),
            pltpu.VMEM((chunks, n_ctx, own_len, LANES), BF16),
            pltpu.VMEM((vocab, length), BF16),
            pltpu.VMEM((chans, length), F32),
            pltpu.VMEM((chans, length), F32),
            pltpu.VMEM((chans, length), F32),
            pltpu.VMEM((chans, length), F32),
            pltpu.VMEM((LANES, chans), F32),
            pltpu.VMEM((chans, LANES), F32),
            pltpu.VMEM((chunks, n_ctx, own_len, LANES), BF16),
            pltpu.VMEM((chunks, n_ctx, own_len, LANES), BF16),
            pltpu.VMEM((groups, length), F32),
            pltpu.VMEM((chans, LANES), F32),
            pltpu.VMEM((chunks, per * n_dp, 8, LANES), F32),
            pltpu.VMEM((chunks, n_dp, per, 8, LANES), F32),
            pltpu.VMEM((chunks, n_dp, per, 8, LANES), F32),
            pltpu.VMEM((chunks, n_ctx, streams, 8, LANES), F32),
            pltpu.VMEM((groups, length), F32),
            pltpu.VMEM((streams, taps, chans), F32),
            dma, dma((3,)), dma((chunks,)), dma((2, chunks)),
            dma((n_ctx,)), dma((n_ctx,)),
            dma((chunks, n_ctx)), dma((chunks, n_ctx)),
            dma((2, chunks, n_ctx)), dma((2, chunks, n_ctx)),
            dma((chunks, n_dp)), dma((chunks, n_dp)), dma((chunks, n_dp)), dma((chunks, n_dp)),
            dma((chunks, n_ctx)), dma((chunks, n_ctx)),
        ],
        compiler_params=pltpu.CompilerParams(
            vmem_limit_bytes=VMEM_LIMIT, collective_id=0, has_side_effects=True),
        name="hyena",
    )(tokens, embedding, cotangent, long_filter, short_filter)
    return tuple(parts)


def solution(mesh):
    in_specs = (P("dp", "ctx"), P(), P("dp", "ctx", None), P("ctx", None), P())
    out_specs = (P("dp", "ctx", None), P("dp", "ctx", None), P("ctx", None), P())
    return jax.shard_map(
        on_device, mesh=mesh, in_specs=in_specs, out_specs=out_specs, check_vma=False
    )
```
